32 devices in a mesh: rep: 4 (over z), expert: 8 (over y, x, core).
Axes of the slice: x: 2, y: 2, z: 4, core: 2. Of those that a mesh axis runs over, the one named last changes fastest.
Arguments:
- tokens: bfloat16 [4096, 2048], P(('rep', 'expert')), may hold values from -6 to 6
- norm_gain: float32 [2048], replicated, may hold values from 0.1 to 1.9
- router: bfloat16 [2048, 32], P('rep'), may hold values from -0.125 to 0.125
- routes: int32 [4096, 8], P(('rep', 'expert')), may hold values from 0 to 31, all different within a row; in each aligned block of 128 rows (0 to 127, 128 to 255, ...) at most 48 rows name the same one
- placement: int32 [32], replicated, may hold values from 0 to 31, each once
- w_gate: bfloat16 [32, 2048, 768], P(('rep', 'expert')), may hold values from -0.125 to 0.125
- w_up: bfloat16 [32, 2048, 768], P(('rep', 'expert')), may hold values from -0.125 to 0.125
- w_down: bfloat16 [32, 768, 2048], P(('rep', 'expert')), may hold values from -0.21875 to 0.21875
Outputs:
- moe_out: bfloat16 [4096, 2048], P(('rep', 'expert'))
The draws below stay inside these ranges and needn't reach their ends.
Inputs may be any that keep to these rules, and one draw needn't show every extreme that they name: `routes`: each token's 8 experts differ. Among the 128 tokens of one device at most 48 rows name any one expert, and in some devices' rows one expert is named exactly 48 times. `placement`: A permutation. Weight slot s lies on the device numbered s over rep then expert.
All inputs are finite; a program needn't handle non-finite values.
Results may differ from the reference program's by a relative error of at most 0.0075.
Values may be sent and summed in bfloat16 or wider, within the bound.
No kernel may reach another device: no remote copies, remote signals or barrier semaphores. Data moves between devices by JAX's collectives and lax.ppermute only.
A program may use at most 128 MiB of HBM per device.

```python
import math
import jax
import jax.numpy as jnp
import numpy as np
from jax import lax

D = 2048
FF = 768
TOP = 8
TOK_DEV = 128
EXPERTS = 32
TOKENS = 4096
CAP = 48
N_REP = 4
N_EXPERT = 8


def levels(rng, shape, pieces, low, top_value):
    level, own = 1.0, jax.random.fold_in(rng, 6)
    for axis_at, parts in pieces:
        steps = jnp.exp(jax.random.uniform(jax.random.fold_in(own, axis_at), (parts,), jnp.float32, low / len(pieces), top_value / len(pieces)))
        level = level * jnp.repeat(steps, shape[axis_at] // parts).reshape([-1 if axis == axis_at else 1 for axis in range(len(shape))])
    return level


def routed_block(rng, own, number, rows, amount, top, reach, slope):
    ranking = jax.random.permutation(rng, amount)
    packed, ordinary = portions_of(amount, rows * top, reach, slope, True), portions_of(amount, rows * top, reach, slope, False)
    places = jnp.arange(amount)

    def named(sizes, rotation):
        used = int((sizes > 0).sum())
        fixed = max(1, used // 4)
        passed = fixed + (places - fixed + rotation * (used - fixed)) % max(1, amount - fixed)
        return jnp.zeros((amount,), jnp.int32).at[ranking[jnp.where(places < fixed, places, passed)]].set(jnp.asarray(sizes, jnp.int32))

    sizes = jnp.where(number % 4 == 0, named(packed, number // 4), named(ordinary, number - number // 4 - 1))
    mixed = jax.random.permutation(jax.random.fold_in(own, 3), amount)
    source_of, taker = mixed[0:amount // 2 * 2:2], mixed[1:amount // 2 * 2:2]
    slack = jnp.minimum(sizes[source_of] - 1, reach - sizes[taker]) // 2
    slack = jnp.where((source_of == ranking[0]) | (taker == ranking[0]) | (sizes[taker] == 0), 0, jnp.maximum(slack, 0))
    passed = jax.random.randint(jax.random.fold_in(own, 4), (amount // 2,), 0, 1 << 20) % (slack + 1)
    sizes = sizes.at[source_of].add(-passed).at[taker].add(passed)
    items = jnp.searchsorted(jnp.cumsum(sizes), jnp.arange(rows * top), side="right").astype(jnp.int32)
    grid = items.reshape(top, rows).T
    grid = grid[jax.random.permutation(jax.random.fold_in(own, 1), rows)]
    rotation = jax.random.randint(jax.random.fold_in(own, 2), (rows, 1), 0, top)
    return jnp.take_along_axis(grid, (jnp.arange(top)[None, :] + rotation) % top, axis=1)


def portions_of(amount, total, most, lean, full):
    portions = [(1 << 20) // math.isqrt(standing ** lean) + 1 for standing in range(1, amount + 1)]
    largest = most if full else min(most, max(-(-total // amount), total * portions[0] // sum(portions)))
    least = 1 if total - largest >= amount - 1 else 0
    counts, rest = [largest] + [least] * (amount - 1), total - largest - least * (amount - 1)
    while rest > 0:
        candidates = [i for i in range(1, amount) if counts[i] < largest] or [i for i in range(1, amount) if counts[i] < most]
        mass, left = sum([portions[i] for i in candidates]), rest
        for i in candidates:
            more = min(most - counts[i], max(1, left * portions[i] // mass), rest)
            counts[i] = counts[i] + more
            rest = rest - more
    return np.array(counts)


def bell_draw(rng, shape, deviation, reach, split=(), held_as=jnp.bfloat16):
    values = deviation * jax.random.normal(rng, shape, jnp.float32)
    if split:
        values = values * levels(rng, shape, split, -0.22, 0.18)
    return jnp.clip(values, -reach, reach).astype(held_as)


def setup_inputs(seed: int = 0) -> dict:
    key_list = jax.random.split(jax.random.key(seed), 9)
    tokens = bell_draw(key_list[0], (TOKENS, D), 1.0, 6.0, ((0, 32),))
    norm_gain = jnp.clip(1.0 + 0.18 * jax.random.normal(key_list[1], (D,), jnp.float32), 0.1, 1.9)
    router = bell_draw(key_list[2], (D, EXPERTS), D ** -0.5, 0.125, ((0, 4),))
    routes_keys = jax.random.split(jax.random.fold_in(key_list[3], 1), TOKENS // TOK_DEV)
    routes_turns = jax.random.permutation(jax.random.fold_in(key_list[3], 3), TOKENS // TOK_DEV)
    routes = jax.vmap(lambda own, number: routed_block(jax.random.fold_in(key_list[3], 2), own, number, TOK_DEV, EXPERTS, TOP, CAP, 2))(routes_keys, routes_turns).reshape((TOKENS, TOP))
    placement = jax.random.permutation(key_list[4], EXPERTS).astype(jnp.int32)
    w_gate = bell_draw(key_list[5], (EXPERTS, D, FF), D ** -0.5, 0.125, ((0, 32),))
    w_up = bell_draw(key_list[6], (EXPERTS, D, FF), D ** -0.5, 0.125, ((0, 32),))
    w_down = bell_draw(key_list[7], (EXPERTS, FF, D), FF ** -0.5, 0.21875, ((0, 32),))
    return dict(tokens=tokens, norm_gain=norm_gain, router=router, routes=routes, placement=placement, w_gate=w_gate, w_up=w_up, w_down=w_down)


def reference(tokens, norm_gain, router, routes, placement, w_gate, w_up, w_down):
    values = tokens.astype(jnp.float32)
    scale = lax.rsqrt(lax.optimization_barrier(jnp.mean(values * values, axis=-1, keepdims=True)) + 1e-06)
    normed = (values * scale * norm_gain[None, :]).astype(jnp.bfloat16)
    logits = jnp.dot(normed, router, preferred_element_type=jnp.float32)
    picked = jnp.take_along_axis(logits, routes, axis=1)
    powers = jnp.exp(picked)
    shares = (powers / lax.optimization_barrier(jnp.sum(powers, axis=1, keepdims=True))).reshape(-1)
    flat_routes = routes.reshape(-1)
    bound = N_REP * N_EXPERT * CAP

    def one_expert(accumulated, expert_id):
        chosen = flat_routes == expert_id
        members = jnp.nonzero(chosen, size=bound, fill_value=0)[0].astype(jnp.int32)
        live_mask = (jnp.arange(bound, dtype=jnp.int32) < jnp.sum(chosen.astype(jnp.int32))).astype(jnp.float32)
        slot_index = placement[expert_id]
        token_index = members // TOP
        selected = normed[token_index]
        gate_proj = jnp.dot(selected, w_gate[slot_index], preferred_element_type=jnp.float32)
        up_proj = jnp.dot(selected, w_up[slot_index], preferred_element_type=jnp.float32)
        hidden = (jax.nn.silu(gate_proj) * up_proj).astype(jnp.bfloat16)
        output_row = jnp.dot(hidden, w_down[slot_index], preferred_element_type=jnp.float32).astype(jnp.bfloat16)
        output_row = lax.optimization_barrier(output_row).astype(jnp.float32)
        weighted = output_row * (shares[members] * live_mask)[:, None]
        return (accumulated.at[token_index].add(weighted), None)
    start = jnp.zeros((TOKENS, D), jnp.float32)
    total_sum, unused = lax.scan(one_expert, start, jnp.arange(EXPERTS, dtype=jnp.int32))
    return total_sum.astype(jnp.bfloat16)
```

```python
import functools

import jax
import jax.numpy as jnp
from jax import lax
from jax.experimental import pallas as pl
from jax.experimental.pallas import tpu as pltpu
from jax.sharding import PartitionSpec as P

BF16, F32, I32 = jnp.bfloat16, jnp.float32, jnp.int32
CORES = 2
Y_SIZE = 2
HALVES = 2
MIB = 1 << 20
SMEM = pl.BlockSpec(memory_space=pltpu.SMEM)
VMEM = pl.BlockSpec(memory_space=pltpu.VMEM)
HBM = pl.BlockSpec(memory_space=pltpu.HBM)


def round_up(number, step):
    return -(-number // step) * step


def took(microseconds):
    return pl.CostEstimate(flops=int(microseconds * 1e9), bytes_accessed=0, transcendentals=0)


def params():
    return pltpu.CompilerParams(vmem_limit_bytes=12 * MIB)


def pack_kernel(piece, tokens, gain, routes, router, out_ref):
    rows, width = tokens.shape
    top = routes.shape[0]
    depth = router.shape[1]
    extra = out_ref.shape[0] - rows
    values = tokens[...].astype(F32)
    scale = lax.rsqrt(jnp.mean(values * values, axis=-1, keepdims=True) + 1e-06)
    out_ref[:rows, :] = (values * scale * gain[...]).astype(BF16)
    spread = jnp.concatenate(
        [router[q * piece : (q + 1) * piece, :].astype(F32) for q in range(width // depth)], axis=1
    )
    parts = [jnp.concatenate([routes[...].astype(F32), jnp.zeros((top, width - rows), F32)], axis=1), spread]
    if extra > top + piece:
        parts.insert(1, jnp.zeros((extra - top - piece, width), F32))
    out_ref[rows:, :] = jnp.concatenate(parts, axis=0).astype(BF16)


def router_kernel(rows, piece, plane_ref, *refs):
    blocks, out_ref = refs[:-1], refs[-1]
    pieces = len(blocks)
    depth = out_ref.shape[1] // pieces
    for d, block in enumerate(blocks):
        start = pl.multiple_of(lax.rem(plane_ref[0] - d + pieces, pieces) * depth, depth)
        last = block[rows:, :].astype(F32)[-piece:]
        out_ref[:, pl.ds(start, depth)] = jnp.concatenate(
            [last[:, q * depth : (q + 1) * depth] for q in range(pieces)], axis=0
        ).astype(BF16)


def membership(routes, experts, rows):
    names = lax.broadcasted_iota(I32, (experts, rows), 0).astype(F32)
    member = names == routes[0:1, :]
    for k in range(1, routes.shape[0]):
        member = member | (names == routes[k : k + 1, :])
    return member


def positions(member, groups_ref, rows):
    mine = jnp.dot(
        groups_ref[...].astype(BF16), jnp.where(member, 1.0, 0.0).astype(BF16), preferred_element_type=F32
    )
    earlier = lax.broadcasted_iota(I32, (rows, rows), 0) < lax.broadcasted_iota(I32, (rows, rows), 1)
    rank = jnp.dot(
        mine.astype(BF16), jnp.where(earlier, 1.0, 0.0).astype(BF16), preferred_element_type=F32
    )
    return jnp.where(mine > 0, rank, -1.0)


def select_kernel(rows, cap, top, groups_ref, *refs):
    groups, experts = groups_ref.shape
    blocks, outs = refs[:-groups], refs[-groups:]
    slot = lax.broadcasted_iota(I32, (cap, rows), 0).astype(F32)
    for i, block in enumerate(blocks):
        routes = block[rows : rows + 16, :rows].astype(F32)[:top]
        place = positions(membership(routes, experts, rows), groups_ref, rows)
        pick = jnp.concatenate(
            [jnp.where(slot == place[j : j + 1, :], 1.0, 0.0) for j in range(groups)], axis=0
        ).astype(BF16)
        found = jnp.dot(pick, block[:rows, :], preferred_element_type=F32).astype(BF16)
        for j in range(groups):
            outs[j][i * cap : (i + 1) * cap, :] = found[j * cap : (j + 1) * cap, :]


def experts_kernel(groups, *refs):
    ins, (gate_ref, up_ref, down_ref) = refs[:groups], refs[groups : groups + 3]
    outs, (stacked,) = refs[groups + 3 : -1], refs[-1:]
    size = ins[0].shape[0]
    hidden_width = gate_ref.shape[2]
    for j in range(groups):
        stacked[j * size : (j + 1) * size, :] = ins[j][...]
    gate = jnp.dot(stacked[...], gate_ref[0], preferred_element_type=F32)
    up = jnp.dot(stacked[...], up_ref[0], preferred_element_type=F32)
    hidden = (gate / (1.0 + jnp.exp(-gate)) * up).astype(BF16)
    product = jnp.dot(hidden, down_ref[0], preferred_element_type=F32).astype(BF16)
    for j in range(groups):
        outs[j][...] = product[j * size : (j + 1) * size, :]


def combine_kernel(rows, cap, top, dense, halves, groups_ref, router_ref, *refs):
    groups, experts = groups_ref.shape
    blocks, results, outs = refs[:dense], refs[dense : dense + groups], refs[dense + groups :]
    slot = lax.broadcasted_iota(I32, (cap, rows), 0).astype(F32)
    for i, block in enumerate(blocks):
        routes = block[rows : rows + 16, :rows].astype(F32)[:top]
        member = membership(routes, experts, rows)
        place = positions(member, groups_ref, rows)
        logits = lax.dot_general(
            router_ref[...], block[:rows, :], (((1,), (1,)), ((), ())), preferred_element_type=F32
        )
        powers = jnp.where(member, jnp.exp(logits), 0.0)
        shares = powers / jnp.sum(powers, axis=0, keepdims=True)
        own = jnp.dot(
            groups_ref[...], shares, preferred_element_type=F32, precision=lax.Precision.HIGHEST
        )
        weights = jnp.concatenate(
            [jnp.where(slot == place[j : j + 1, :], own[j : j + 1, :], 0.0) for j in range(groups)], axis=0
        )
        coarse = weights.astype(BF16)
        fine = (weights - coarse.astype(F32)).astype(BF16)
        found = jnp.concatenate(
            [result[i * cap : (i + 1) * cap, :] for result in results], axis=0
        )
        down = (((0,), (0,)), ((), ()))
        summed = lax.dot_general(coarse, found, down, preferred_element_type=F32)
        summed = summed + lax.dot_general(fine, found, down, preferred_element_type=F32)
        parts = outs[:1] if i == 0 else outs[1 + (i - 1) * halves : 1 + i * halves]
        size = rows // len(parts)
        for h, part in enumerate(parts):
            part[...] = summed[h * size : (h + 1) * size].astype(part.dtype)


def add_kernel(starts, own, *refs):
    out_ref = refs[-1]
    cuts = sorted(set(starts)) + [own.shape[0]]
    for low, high in zip(cuts[:-1], cuts[1:]):
        part = own[low:high, :]
        for start, ref in zip(starts, refs[:-1]):
            if start <= low < start + ref.shape[0]:
                part = part + ref[low - start : high - start, :].astype(F32)
        out_ref[low:high, :] = part.astype(BF16)


def per_device(tokens, norm_gain, router, routes, placement, w_gate, w_up, w_down):
    rows, width = tokens.shape
    top = routes.shape[1]
    experts = placement.shape[0]
    reps = lax.axis_size("rep")
    owners = lax.axis_size("expert")
    x_size = owners // (Y_SIZE * CORES)
    cap = round_up(3 * rows * top // (2 * experts), 16)
    plane = lax.axis_index("rep")
    owner = lax.axis_index("expert")
    depth = router.shape[0]
    piece = experts // reps
    extra = round_up(top + piece, 16)
    mixed = x_size == Y_SIZE
    dense = x_size
    steps = [(by, core_by) for by in range(Y_SIZE) for core_by in range(CORES)]

    def moved(y, x, core, by, core_by, along_x):
        if along_x:
            x = (x + by) % x_size
        else:
            y = (y + by) % Y_SIZE
        return (y * x_size + x) * CORES + (core ^ core_by)

    def shift_owner(array, by, core_by, is_dense):
        pairs = []
        for y in range(Y_SIZE):
            for x in range(x_size):
                for core in range(CORES):
                    along_x = is_dense ^ (mixed and core == 1)
                    there = moved(y, x, core, abs(by), core_by, along_x)
                    pairs.append(((y * x_size + x) * CORES + core, there))
        return lax.ppermute(array, "expert", pairs if by >= 0 else [(b, a) for a, b in pairs])

    def shift_plane(array, by):
        return lax.ppermute(array, "rep", [(r, (r + by) % reps) for r in range(reps)])

    core = owner % CORES
    x_at = owner // CORES % x_size
    y_at = owner // CORES // x_size
    slots = []
    for by, core_by in steps:
        there = moved(y_at, x_at, core, by, core_by, False)
        if mixed:
            there = jnp.where(core == 1, moved(y_at, x_at, core, by, core_by, True), there)
        slots.append(plane * owners + there)
    groups = (placement[None, :] == jnp.stack(slots)[:, None]).astype(F32)

    shapes = [(rows, width), (1, width), (top, rows), (experts, depth)]
    packed = pl.pallas_call(
        functools.partial(pack_kernel, piece),
        out_shape=jax.ShapeDtypeStruct((rows + extra, width), BF16),
        in_specs=[pl.BlockSpec(shape, lambda i: (0, 0)) for shape in shapes],
        out_specs=VMEM,
        grid=(1,),
        compiler_params=params(),
        name="pack",
    )(tokens, norm_gain.reshape(1, width), routes.T, router.T)

    def after(array, *others):
        return lax.optimization_barrier((array, *others))[0]

    def after_all(arrays, *others):
        return lax.optimization_barrier((tuple(arrays), *others))[0]

    def select(blocks):
        return pl.pallas_call(
            functools.partial(select_kernel, rows, cap, top),
            out_shape=[jax.ShapeDtypeStruct((dense * cap, width), BF16)] * len(steps),
            in_specs=[VMEM] * (1 + dense),
            out_specs=[VMEM] * len(steps),
            compiler_params=params(),
            cost_estimate=took(1),
            name="select",
        )(groups, *blocks)

    def send_blocks(block):
        return [block] + [shift_owner(block, by, 0, True) for by in range(1, dense)]

    def send_rows(sent):
        return [sent[0]] + [shift_owner(sent[j], *steps[j], False) for j in range(1, len(steps))]

    def whole_router(sources):
        return pl.pallas_call(
            functools.partial(router_kernel, rows, piece),
            out_shape=jax.ShapeDtypeStruct((experts, width), BF16),
            in_specs=[SMEM] + [VMEM] * reps,
            out_specs=VMEM,
            compiler_params=params(),
            cost_estimate=took(1),
            name="router",
        )(plane.reshape(1), *sources)

    def apply_experts(here):
        size, count = here[0].shape[0], len(here)
        results = pl.pallas_call(
            functools.partial(experts_kernel, count),
            out_shape=[jax.ShapeDtypeStruct((size, width), BF16)] * count,
            in_specs=[VMEM] * (count + 3),
            out_specs=[VMEM] * count,
            scratch_shapes=[pltpu.VMEM((size * count, width), BF16)],
            compiler_params=params(),
            cost_estimate=took(4),
            name="experts",
        )(*here, w_gate, w_up, w_down)
        return results

    def shift_back(array, by, core_by, is_dense):
        pairs = []
        for y in range(Y_SIZE):
            for x in range(x_size):
                for core_at in range(CORES):
                    along_x = is_dense ^ (mixed and core_at == 1)
                    there = moved(y, x, core_at, by, core_by, along_x)
                    pairs.append((there, (y * x_size + x) * CORES + core_at))
        return lax.ppermute(array, "expert", pairs)

    def combine(blocks, back, router_full, halves):
        sums = pl.pallas_call(
            functools.partial(combine_kernel, rows, cap, top, dense, halves),
            out_shape=[jax.ShapeDtypeStruct((rows, width), F32)]
            + [jax.ShapeDtypeStruct((rows // halves, width), BF16)] * (halves * (dense - 1)),
            in_specs=[VMEM] * (2 + dense + len(steps)),
            out_specs=[VMEM] * (1 + halves * (dense - 1)),
            compiler_params=params(),
            cost_estimate=took(2),
            name="combine",
        )(groups, router_full, *blocks, *back)
        return sums

    def return_sums(sums):
        halves = (len(sums) - 1) // (dense - 1)
        return [sums[0]] + [
            [shift_back(sums[1 + by * halves + h], by + 1, 0, True) for by in range(dense - 1)]
            for h in range(halves)
        ]

    def add_up(own, *lists):
        starts, parts = [], []
        for pieces in lists:
            size = rows // len(pieces)
            starts += [h * size for h in range(len(pieces))]
            parts += pieces
        return pl.pallas_call(
            functools.partial(add_kernel, starts),
            out_shape=jax.ShapeDtypeStruct((rows, width), BF16),
            in_specs=[VMEM] * (1 + len(parts)),
            out_specs=VMEM,
            compiler_params=params(),
            cost_estimate=took(1),
            name="add",
        )(own, *parts)

    last = reps - 1
    blocks = [send_blocks(packed)]
    sources = [packed]
    for _ in range(last):
        sources.append(shift_plane(sources[-1], 1))
    sent = select(blocks[0])
    here = send_rows(sent)
    mark = sent[0]
    back, travelling = [], []

    def combine_chunk(i, halves, *others):
        back[i][0] = after(back[i][0], *others)
        sums = combine(blocks[i], back[i], router_full, halves)
        return sums[0], return_sums(sums)

    def add_chunk(sums, *others):
        own = after(sums[0], *others)
        lists = [list(column) for column in zip(*sums[1:])]
        part = add_up(own, *lists, *([travelling] if travelling else []))
        travelling[:] = [shift_plane(part, 1)]
        return part

    def send_back(results, *others):
        back = [results[0]]
        for j in range(1, len(steps)):
            rows_back = after(results[j], back[1], *others) if others and j > 1 else results[j]
            back.append(shift_back(rows_back, *steps[j], False))
        return back

    sums = None
    blocks.append(send_blocks(after(sources[1], *here[1:3])))
    for i in range(reps):
        arrived = here
        if 0 < i < last:
            blocks[i + 1][0] = after(blocks[i + 1][0], mark, *sources[i + 2 : i + 3])
            sent = select(blocks[i + 1])
            mark = sent[0]
            here = send_rows([sent[0]] + [after(rows_out, *arrived) for rows_out in sent[1:]])
            if i + 2 <= last:
                blocks.append(send_blocks(after(sources[i + 2], mark, *arrived)))
        if i == 2:
            router_full = whole_router([after(sources[0], mark)] + sources[1:])
        if 1 < i < last:
            mark, sums = combine_chunk(i - 1, 1, mark)
        arrived[0] = after(arrived[0], mark, *(back[i - 1][1:] if 1 < i < last else []))
        results = apply_experts(arrived)
        back.append(send_back(results) if 0 < i < last else list(results))
        mark = results[0]
        if i == 0:
            blocks[1][0] = after(blocks[1][0], mark)
            sent = select(blocks[1])
            mark = sent[0]
            here = send_rows(sent)
            blocks.append(send_blocks(after(sources[2], mark, here[1])))
        if i == last:
            mark = add_chunk(sums, mark)
            mark, sums = combine_chunk(i - 1, HALVES, mark)
            back[last] = send_back(results, mark)
    mark = add_chunk(sums, mark)
    mark, sums = combine_chunk(last, HALVES, mark)
    back[0] = send_back([back[0][0]] + [after(x, mark) for x in back[0][1:]])
    mark = add_chunk(sums)
    back[0][0] = after(back[0][0], mark)
    own = return_sums(combine(blocks[0], back[0], router_full, HALVES))
    return add_up(own[0], *[list(column) for column in zip(*own[1:])], travelling)


def solution(mesh):
    placed = (
        P(("rep", "expert"), None),
        P(),
        P("rep", None),
        P(("rep", "expert"), None),
        P(),
        P(("rep", "expert"), None, None),
        P(("rep", "expert"), None, None),
        P(("rep", "expert"), None, None),
    )
    return jax.shard_map(
        per_device,
        mesh=mesh,
        in_specs=placed,
        out_specs=P(("rep", "expert"), None),
        check_vma=False,
    )
```

```python
import functools

import jax
import jax.numpy as jnp
from jax import lax
from jax.experimental import pallas as pl
from jax.experimental.pallas import tpu as pltpu
from jax.sharding import PartitionSpec as P

BF16, F32, I32 = jnp.bfloat16, jnp.float32, jnp.int32
CORES = 2
Y_SIZE = 2
HALVES = 2
MIB = 1 << 20
SMEM = pl.BlockSpec(memory_space=pltpu.SMEM)
VMEM = pl.BlockSpec(memory_space=pltpu.VMEM)
HBM = pl.BlockSpec(memory_space=pltpu.HBM)


def round_up(number, step):
    return -(-number // step) * step


def took(microseconds):
    return pl.CostEstimate(flops=int(microseconds * 1e9), bytes_accessed=0, transcendentals=0)


def params():
    return pltpu.CompilerParams(vmem_limit_bytes=12 * MIB)


def pack_kernel(piece, tokens, gain, routes, router, out_ref):
    rows, width = tokens.shape
    top = routes.shape[0]
    depth = router.shape[1]
    extra = out_ref.shape[0] - rows
    values = tokens[...].astype(F32)
    scale = lax.rsqrt(jnp.mean(values * values, axis=-1, keepdims=True) + 1e-06)
    out_ref[:rows, :] = (values * scale * gain[...]).astype(BF16)
    spread = jnp.concatenate(
        [router[q * piece : (q + 1) * piece, :].astype(F32) for q in range(width // depth)], axis=1
    )
    parts = [jnp.concatenate([routes[...].astype(F32), jnp.zeros((top, width - rows), F32)], axis=1), spread]
    if extra > top + piece:
        parts.insert(1, jnp.zeros((extra - top - piece, width), F32))
    out_ref[rows:, :] = jnp.concatenate(parts, axis=0).astype(BF16)


def router_kernel(rows, piece, plane_ref, *refs):
    blocks, out_ref = refs[:-1], refs[-1]
    pieces = len(blocks)
    depth = out_ref.shape[1] // pieces
    for d, block in enumerate(blocks):
        start = pl.multiple_of(lax.rem(plane_ref[0] - d + pieces, pieces) * depth, depth)
        last = block[rows:, :].astype(F32)[-piece:]
        out_ref[:, pl.ds(start, depth)] = jnp.concatenate(
            [last[:, q * depth : (q + 1) * depth] for q in range(pieces)], axis=0
        ).astype(BF16)


def membership(routes, experts, rows):
    names = lax.broadcasted_iota(I32, (experts, rows), 0).astype(F32)
    member = names == routes[0:1, :]
    for k in range(1, routes.shape[0]):
        member = member | (names == routes[k : k + 1, :])
    return member


def positions(member, groups_ref, rows):
    mine = jnp.dot(
        groups_ref[...].astype(BF16), jnp.where(member, 1.0, 0.0).astype(BF16), preferred_element_type=F32
    )
    earlier = lax.broadcasted_iota(I32, (rows, rows), 0) < lax.broadcasted_iota(I32, (rows, rows), 1)
    rank = jnp.dot(
        mine.astype(BF16), jnp.where(earlier, 1.0, 0.0).astype(BF16), preferred_element_type=F32
    )
    return jnp.where(mine > 0, rank, -1.0)


def select_kernel(rows, cap, top, groups_ref, *refs):
    groups, experts = groups_ref.shape
    blocks, outs = refs[:-groups], refs[-groups:]
    slot = lax.broadcasted_iota(I32, (cap, rows), 0).astype(F32)
    for i, block in enumerate(blocks):
        routes = block[rows : rows + 16, :rows].astype(F32)[:top]
        place = positions(membership(routes, experts, rows), groups_ref, rows)
        pick = jnp.concatenate(
            [jnp.where(slot == place[j : j + 1, :], 1.0, 0.0) for j in range(groups)], axis=0
        ).astype(BF16)
        found = jnp.dot(pick, block[:rows, :], preferred_element_type=F32).astype(BF16)
        for j in range(groups):
            outs[j][i * cap : (i + 1) * cap, :] = found[j * cap : (j + 1) * cap, :]


def experts_kernel(groups, *refs):
    ins, (gate_ref, up_ref, down_ref) = refs[:groups], refs[groups : groups + 3]
    outs, (stacked,) = refs[groups + 3 : -1], refs[-1:]
    size = ins[0].shape[0]
    hidden_width = gate_ref.shape[2]
    for j in range(groups):
        stacked[j * size : (j + 1) * size, :] = ins[j][...]
    gate = jnp.dot(stacked[...], gate_ref[0], preferred_element_type=F32)
    up = jnp.dot(stacked[...], up_ref[0], preferred_element_type=F32)
    hidden = (gate / (1.0 + jnp.exp(-gate)) * up).astype(BF16)
    product = jnp.dot(hidden, down_ref[0], preferred_element_type=F32).astype(BF16)
    for j in range(groups):
        outs[j][...] = product[j * size : (j + 1) * size, :]


def combine_kernel(rows, cap, top, dense, halves, groups_ref, router_ref, *refs):
    groups, experts = groups_ref.shape
    blocks, results, outs = refs[:dense], refs[dense : dense + groups], refs[dense + groups :]
    slot = lax.broadcasted_iota(I32, (cap, rows), 0).astype(F32)
    for i, block in enumerate(blocks):
        routes = block[rows : rows + 16, :rows].astype(F32)[:top]
        member = membership(routes, experts, rows)
        place = positions(member, groups_ref, rows)
        logits = lax.dot_general(
            router_ref[...], block[:rows, :], (((1,), (1,)), ((), ())), preferred_element_type=F32
        )
        powers = jnp.where(member, jnp.exp(logits), 0.0)
        shares = powers / jnp.sum(powers, axis=0, keepdims=True)
        own = jnp.dot(
            groups_ref[...], shares, preferred_element_type=F32, precision=lax.Precision.HIGHEST
        )
        weights = jnp.concatenate(
            [jnp.where(slot == place[j : j + 1, :], own[j : j + 1, :], 0.0) for j in range(groups)], axis=0
        )
        coarse = weights.astype(BF16)
        fine = (weights - coarse.astype(F32)).astype(BF16)
        found = jnp.concatenate(
            [result[i * cap : (i + 1) * cap, :] for result in results], axis=0
        )
        down = (((0,), (0,)), ((), ()))
        summed = lax.dot_general(coarse, found, down, preferred_element_type=F32)
        summed = summed + lax.dot_general(fine, found, down, preferred_element_type=F32)
        parts = outs[:1] if i == 0 else outs[1 + (i - 1) * halves : 1 + i * halves]
        size = rows // len(parts)
        for h, part in enumerate(parts):
            part[...] = summed[h * size : (h + 1) * size].astype(part.dtype)


def add_kernel(starts, own, *refs):
    out_ref = refs[-1]
    cuts = sorted(set(starts)) + [own.shape[0]]
    for low, high in zip(cuts[:-1], cuts[1:]):
        part = own[low:high, :]
        for start, ref in zip(starts, refs[:-1]):
            if start <= low < start + ref.shape[0]:
                part = part + ref[low - start : high - start, :].astype(F32)
        out_ref[low:high, :] = part.astype(BF16)


def per_device(tokens, norm_gain, router, routes, placement, w_gate, w_up, w_down):
    rows, width = tokens.shape
    top = routes.shape[1]
    experts = placement.shape[0]
    reps = lax.axis_size("rep")
    owners = lax.axis_size("expert")
    x_size = owners // (Y_SIZE * CORES)
    cap = round_up(3 * rows * top // (2 * experts), 16)
    plane = lax.axis_index("rep")
    owner = lax.axis_index("expert")
    depth = router.shape[0]
    piece = experts // reps
    extra = round_up(top + piece, 16)
    mixed = x_size == Y_SIZE
    dense = x_size
    steps = [(by, core_by) for by in range(Y_SIZE) for core_by in range(CORES)]

    def moved(y, x, core, by, core_by, along_x):
        if along_x:
            x = (x + by) % x_size
        else:
            y = (y + by) % Y_SIZE
        return (y * x_size + x) * CORES + (core ^ core_by)

    def shift_owner(array, by, core_by, is_dense):
        pairs = []
        for y in range(Y_SIZE):
            for x in range(x_size):
                for core in range(CORES):
                    along_x = is_dense ^ (mixed and core == 1)
                    there = moved(y, x, core, abs(by), core_by, along_x)
                    pairs.append(((y * x_size + x) * CORES + core, there))
        return lax.ppermute(array, "expert", pairs if by >= 0 else [(b, a) for a, b in pairs])

    def shift_plane(array, by):
        return lax.ppermute(array, "rep", [(r, (r + by) % reps) for r in range(reps)])

    core = owner % CORES
    x_at = owner // CORES % x_size
    y_at = owner // CORES // x_size
    slots = []
    for by, core_by in steps:
        there = moved(y_at, x_at, core, by, core_by, False)
        if mixed:
            there = jnp.where(core == 1, moved(y_at, x_at, core, by, core_by, True), there)
        slots.append(plane * owners + there)
    groups = (placement[None, :] == jnp.stack(slots)[:, None]).astype(F32)

    shapes = [(rows, width), (1, width), (top, rows), (experts, depth)]
    packed = pl.pallas_call(
        functools.partial(pack_kernel, piece),
        out_shape=jax.ShapeDtypeStruct((rows + extra, width), BF16),
        in_specs=[pl.BlockSpec(shape, lambda i: (0, 0)) for shape in shapes],
        out_specs=VMEM,
        grid=(1,),
        compiler_params=params(),
        name="pack",
    )(tokens, norm_gain.reshape(1, width), routes.T, router.T)

    def after(array, *others):
        return lax.optimization_barrier((array, *others))[0]

    def after_all(arrays, *others):
        return lax.optimization_barrier((tuple(arrays), *others))[0]

    def select(blocks):
        return pl.pallas_call(
            functools.partial(select_kernel, rows, cap, top),
            out_shape=[jax.ShapeDtypeStruct((dense * cap, width), BF16)] * len(steps),
            in_specs=[VMEM] * (1 + dense),
            out_specs=[VMEM] * len(steps),
            compiler_params=params(),
            cost_estimate=took(1),
            name="select",
        )(groups, *blocks)

    def send_blocks(block):
        return [block] + [shift_owner(block, by, 0, True) for by in range(1, dense)]

    def send_rows(sent):
        return [sent[0]] + [shift_owner(sent[j], *steps[j], False) for j in range(1, len(steps))]

    def whole_router(sources):
        return pl.pallas_call(
            functools.partial(router_kernel, rows, piece),
            out_shape=jax.ShapeDtypeStruct((experts, width), BF16),
            in_specs=[SMEM] + [VMEM] * reps,
            out_specs=VMEM,
            compiler_params=params(),
            cost_estimate=took(1),
            name="router",
        )(plane.reshape(1), *sources)

    def apply_experts(here):
        size, count = here[0].shape[0], len(here)
        results = pl.pallas_call(
            functools.partial(experts_kernel, count),
            out_shape=[jax.ShapeDtypeStruct((size, width), BF16)] * count,
            in_specs=[VMEM] * (count + 3),
            out_specs=[VMEM] * count,
            scratch_shapes=[pltpu.VMEM((size * count, width), BF16)],
            compiler_params=params(),
            cost_estimate=took(4),
            name="experts",
        )(*here, w_gate, w_up, w_down)
        return results

    def shift_back(array, by, core_by, is_dense):
        pairs = []
        for y in range(Y_SIZE):
            for x in range(x_size):
                for core_at in range(CORES):
                    along_x = is_dense ^ (mixed and core_at == 1)
                    there = moved(y, x, core_at, by, core_by, along_x)
                    pairs.append((there, (y * x_size + x) * CORES + core_at))
        return lax.ppermute(array, "expert", pairs)

    def combine(blocks, back, router_full, halves):
        sums = pl.pallas_call(
            functools.partial(combine_kernel, rows, cap, top, dense, halves),
            out_shape=[jax.ShapeDtypeStruct((rows, width), F32)]
            + [jax.ShapeDtypeStruct((rows // halves, width), BF16)] * (halves * (dense - 1)),
            in_specs=[VMEM] * (2 + dense + len(steps)),
            out_specs=[VMEM] * (1 + halves * (dense - 1)),
            compiler_params=params(),
            cost_estimate=took(2),
            name="combine",
        )(groups, router_full, *blocks, *back)
        return sums

    def return_sums(sums):
        halves = (len(sums) - 1) // (dense - 1)
        return [sums[0]] + [
            [shift_back(sums[1 + by * halves + h], by + 1, 0, True) for by in range(dense - 1)]
            for h in range(halves)
        ]

    def add_up(own, *lists):
        starts, parts = [], []
        for pieces in lists:
            size = rows // len(pieces)
            starts += [h * size for h in range(len(pieces))]
            parts += pieces
        return pl.pallas_call(
            functools.partial(add_kernel, starts),
            out_shape=jax.ShapeDtypeStruct((rows, width), BF16),
            in_specs=[VMEM] * (1 + len(parts)),
            out_specs=VMEM,
            compiler_params=params(),
            cost_estimate=took(1),
            name="add",
        )(own, *parts)

    last = reps - 1
    blocks = [send_blocks(packed)]
    sources = [packed]
    for _ in range(last):
        sources.append(shift_plane(sources[-1], 1))
    sent = select(blocks[0])
    here = send_rows(sent)
    mark = sent[0]
    back, travelling = [], []

    def combine_chunk(i, halves, *others):
        back[i][0] = after(back[i][0], *others)
        sums = combine(blocks[i], back[i], router_full, halves)
        return sums[0], return_sums(sums)

    def add_chunk(sums, *others):
        own = after(sums[0], *others)
        lists = [list(column) for column in zip(*sums[1:])]
        part = add_up(own, *lists, *([travelling] if travelling else []))
        travelling[:] = [shift_plane(part, 1)]
        return part

    def send_back(results, *others):
        back = [results[0]]
        for j in range(1, len(steps)):
            rows_back = after(results[j], back[1], *others[min(j - 2, 1)]) if others and j > 1 else results[j]
            back.append(shift_back(rows_back, *steps[j], False))
        return back

    sums = None
    blocks.append(send_blocks(after(sources[1], *here[1:3])))
    for i in range(reps):
        arrived = here
        if 0 < i < last:
            blocks[i + 1][0] = after(blocks[i + 1][0], mark, *sources[i + 2 : i + 3])
            sent = select(blocks[i + 1])
            mark = sent[0]
            here = send_rows([sent[0]] + [after(rows_out, *arrived) for rows_out in sent[1:]])
            if i + 2 <= last:
                blocks.append(send_blocks(after(sources[i + 2], mark, *arrived)))
        if i == 2:
            router_full = whole_router([after(sources[0], mark)] + sources[1:])
        if 1 < i < last:
            if sums:
                mark = add_chunk(sums, mark)
            mark, sums = combine_chunk(i - 1, 1, mark)
        arrived[0] = after(arrived[0], mark, *(back[i - 1][1:] if 1 < i < last else []))
        results = apply_experts(arrived)
        back.append(send_back(results) if 0 < i < last else list(results))
        mark = results[0]
        if i == 0:
            blocks[1][0] = after(blocks[1][0], mark)
            sent = select(blocks[1])
            mark = sent[0]
            here = send_rows(sent)
            blocks.append(send_blocks(after(sources[2], mark, *here[1:3])))
        if i == last:
            mark = add_chunk(sums, mark)
            mark, sums = combine_chunk(i - 1, HALVES, mark)
            back[last] = send_back(results, [mark], [mark, *sums[1], *travelling])
    mark = add_chunk(sums, mark)
    mark, sums = combine_chunk(last, HALVES, mark)
    back[0] = send_back([back[0][0]] + [after(x, mark) for x in back[0][1:]])
    mark = add_chunk(sums)
    back[0][0] = after(back[0][0], mark)
    own = return_sums(combine(blocks[0], back[0], router_full, HALVES))
    return add_up(own[0], *[list(column) for column in zip(*own[1:])], travelling)


def solution(mesh):
    placed = (
        P(("rep", "expert"), None),
        P(),
        P("rep", None),
        P(("rep", "expert"), None),
        P(),
        P(("rep", "expert"), None, None),
        P(("rep", "expert"), None, None),
        P(("rep", "expert"), None, None),
    )
    return jax.shard_map(
        per_device,
        mesh=mesh,
        in_specs=placed,
        out_specs=P(("rep", "expert"), None),
        check_vma=False,
    )
```

```python
import functools

import jax
import jax.numpy as jnp
from jax import lax
from jax.experimental import pallas as pl
from jax.experimental.pallas import tpu as pltpu
from jax.sharding import PartitionSpec as P

BF16, F32, I32 = jnp.bfloat16, jnp.float32, jnp.int32
CORES = 2
Y_SIZE = 2
HALVES = 2
MIB = 1 << 20
SMEM = pl.BlockSpec(memory_space=pltpu.SMEM)
VMEM = pl.BlockSpec(memory_space=pltpu.VMEM)
HBM = pl.BlockSpec(memory_space=pltpu.HBM)


def round_up(number, step):
    return -(-number // step) * step


def took(microseconds):
    return pl.CostEstimate(flops=int(microseconds * 1e9), bytes_accessed=0, transcendentals=0)


def params():
    return pltpu.CompilerParams(vmem_limit_bytes=12 * MIB)


def pack_kernel(piece, tokens, gain, routes, router, out_ref):
    rows, width = tokens.shape
    top = routes.shape[0]
    depth = router.shape[1]
    extra = out_ref.shape[0] - rows
    values = tokens[...].astype(F32)
    scale = lax.rsqrt(jnp.mean(values * values, axis=-1, keepdims=True) + 1e-06)
    out_ref[:rows, :] = (values * scale * gain[...]).astype(BF16)
    spread = jnp.concatenate(
        [router[q * piece : (q + 1) * piece, :].astype(F32) for q in range(width // depth)], axis=1
    )
    parts = [jnp.concatenate([routes[...].astype(F32), jnp.zeros((top, width - rows), F32)], axis=1), spread]
    if extra > top + piece:
        parts.insert(1, jnp.zeros((extra - top - piece, width), F32))
    out_ref[rows:, :] = jnp.concatenate(parts, axis=0).astype(BF16)


def router_kernel(rows, piece, plane_ref, *refs):
    blocks, out_ref = refs[:-1], refs[-1]
    pieces = len(blocks)
    depth = out_ref.shape[1] // pieces
    for d, block in enumerate(blocks):
        start = pl.multiple_of(lax.rem(plane_ref[0] - d + pieces, pieces) * depth, depth)
        last = block[rows:, :].astype(F32)[-piece:]
        out_ref[:, pl.ds(start, depth)] = jnp.concatenate(
            [last[:, q * depth : (q + 1) * depth] for q in range(pieces)], axis=0
        ).astype(BF16)


def membership(routes, experts, rows):
    names = lax.broadcasted_iota(I32, (experts, rows), 0).astype(F32)
    member = names == routes[0:1, :]
    for k in range(1, routes.shape[0]):
        member = member | (names == routes[k : k + 1, :])
    return member


def positions(member, groups_ref, rows):
    mine = jnp.dot(
        groups_ref[...].astype(BF16), jnp.where(member, 1.0, 0.0).astype(BF16), preferred_element_type=F32
    )
    earlier = lax.broadcasted_iota(I32, (rows, rows), 0) < lax.broadcasted_iota(I32, (rows, rows), 1)
    rank = jnp.dot(
        mine.astype(BF16), jnp.where(earlier, 1.0, 0.0).astype(BF16), preferred_element_type=F32
    )
    return jnp.where(mine > 0, rank, -1.0)


def select_kernel(rows, cap, top, groups_ref, *refs):
    groups, experts = groups_ref.shape
    blocks, outs = refs[:-groups], refs[-groups:]
    slot = lax.broadcasted_iota(I32, (cap, rows), 0).astype(F32)
    for i, block in enumerate(blocks):
        routes = block[rows : rows + 16, :rows].astype(F32)[:top]
        place = positions(membership(routes, experts, rows), groups_ref, rows)
        pick = jnp.concatenate(
            [jnp.where(slot == place[j : j + 1, :], 1.0, 0.0) for j in range(groups)], axis=0
        ).astype(BF16)
        found = jnp.dot(pick, block[:rows, :], preferred_element_type=F32).astype(BF16)
        for j in range(groups):
            outs[j][i * cap : (i + 1) * cap, :] = found[j * cap : (j + 1) * cap, :]


def experts_kernel(groups, *refs):
    ins, (gate_ref, up_ref, down_ref) = refs[:groups], refs[groups : groups + 3]
    outs, (stacked,) = refs[groups + 3 : -1], refs[-1:]
    size = ins[0].shape[0]
    hidden_width = gate_ref.shape[2]
    for j in range(groups):
        stacked[j * size : (j + 1) * size, :] = ins[j][...]
    gate = jnp.dot(stacked[...], gate_ref[0], preferred_element_type=F32)
    up = jnp.dot(stacked[...], up_ref[0], preferred_element_type=F32)
    hidden = (gate / (1.0 + jnp.exp(-gate)) * up).astype(BF16)
    product = jnp.dot(hidden, down_ref[0], preferred_element_type=F32).astype(BF16)
    for j in range(groups):
        outs[j][...] = product[j * size : (j + 1) * size, :]


def combine_kernel(rows, cap, top, dense, halves, groups_ref, router_ref, *refs):
    groups, experts = groups_ref.shape
    blocks, results, outs = refs[:dense], refs[dense : dense + groups], refs[dense + groups :]
    slot = lax.broadcasted_iota(I32, (cap, rows), 0).astype(F32)
    for i, block in enumerate(blocks):
        routes = block[rows : rows + 16, :rows].astype(F32)[:top]
        member = membership(routes, experts, rows)
        place = positions(member, groups_ref, rows)
        logits = lax.dot_general(
            router_ref[...], block[:rows, :], (((1,), (1,)), ((), ())), preferred_element_type=F32
        )
        powers = jnp.where(member, jnp.exp(logits), 0.0)
        shares = powers / jnp.sum(powers, axis=0, keepdims=True)
        own = jnp.dot(
            groups_ref[...], shares, preferred_element_type=F32, precision=lax.Precision.HIGHEST
        )
        weights = jnp.concatenate(
            [jnp.where(slot == place[j : j + 1, :], own[j : j + 1, :], 0.0) for j in range(groups)], axis=0
        )
        coarse = weights.astype(BF16)
        fine = (weights - coarse.astype(F32)).astype(BF16)
        found = jnp.concatenate(
            [result[i * cap : (i + 1) * cap, :] for result in results], axis=0
        )
        down = (((0,), (0,)), ((), ()))
        summed = lax.dot_general(coarse, found, down, preferred_element_type=F32)
        summed = summed + lax.dot_general(fine, found, down, preferred_element_type=F32)
        parts = outs[:1] if i == 0 else outs[1 + (i - 1) * halves : 1 + i * halves]
        size = rows // len(parts)
        for h, part in enumerate(parts):
            part[...] = summed[h * size : (h + 1) * size].astype(part.dtype)


def add_kernel(starts, own, *refs):
    out_ref = refs[-1]
    cuts = sorted(set(starts)) + [own.shape[0]]
    for low, high in zip(cuts[:-1], cuts[1:]):
        part = own[low:high, :]
        for start, ref in zip(starts, refs[:-1]):
            if start <= low < start + ref.shape[0]:
                part = part + ref[low - start : high - start, :].astype(F32)
        out_ref[low:high, :] = part.astype(BF16)


def per_device(tokens, norm_gain, router, routes, placement, w_gate, w_up, w_down):
    rows, width = tokens.shape
    top = routes.shape[1]
    experts = placement.shape[0]
    reps = lax.axis_size("rep")
    owners = lax.axis_size("expert")
    x_size = owners // (Y_SIZE * CORES)
    cap = round_up(3 * rows * top // (2 * experts), 16)
    plane = lax.axis_index("rep")
    owner = lax.axis_index("expert")
    depth = router.shape[0]
    piece = experts // reps
    extra = round_up(top + piece, 16)
    mixed = x_size == Y_SIZE
    dense = x_size
    steps = [(by, core_by) for by in range(Y_SIZE) for core_by in range(CORES)]

    def moved(y, x, core, by, core_by, along_x):
        if along_x:
            x = (x + by) % x_size
        else:
            y = (y + by) % Y_SIZE
        return (y * x_size + x) * CORES + (core ^ core_by)

    def shift_owner(array, by, core_by, is_dense):
        pairs = []
        for y in range(Y_SIZE):
            for x in range(x_size):
                for core in range(CORES):
                    along_x = is_dense ^ (mixed and core == 1)
                    there = moved(y, x, core, abs(by), core_by, along_x)
                    pairs.append(((y * x_size + x) * CORES + core, there))
        return lax.ppermute(array, "expert", pairs if by >= 0 else [(b, a) for a, b in pairs])

    def shift_plane(array, by):
        return lax.ppermute(array, "rep", [(r, (r + by) % reps) for r in range(reps)])

    core = owner % CORES
    x_at = owner // CORES % x_size
    y_at = owner // CORES // x_size
    slots = []
    for by, core_by in steps:
        there = moved(y_at, x_at, core, by, core_by, False)
        if mixed:
            there = jnp.where(core == 1, moved(y_at, x_at, core, by, core_by, True), there)
        slots.append(plane * owners + there)
    groups = (placement[None, :] == jnp.stack(slots)[:, None]).astype(F32)

    shapes = [(rows, width), (1, width), (top, rows), (experts, depth)]
    packed = pl.pallas_call(
        functools.partial(pack_kernel, piece),
        out_shape=jax.ShapeDtypeStruct((rows + extra, width), BF16),
        in_specs=[pl.BlockSpec(shape, lambda i: (0, 0)) for shape in shapes],
        out_specs=VMEM,
        grid=(1,),
        compiler_params=params(),
        name="pack",
    )(tokens, norm_gain.reshape(1, width), routes.T, router.T)

    def after(array, *others):
        return lax.optimization_barrier((array, *others))[0]

    def after_all(arrays, *others):
        return lax.optimization_barrier((tuple(arrays), *others))[0]

    def select(blocks):
        return pl.pallas_call(
            functools.partial(select_kernel, rows, cap, top),
            out_shape=[jax.ShapeDtypeStruct((dense * cap, width), BF16)] * len(steps),
            in_specs=[VMEM] * (1 + dense),
            out_specs=[VMEM] * len(steps),
            compiler_params=params(),
            cost_estimate=took(1),
            name="select",
        )(groups, *blocks)

    def send_blocks(block):
        return [block] + [shift_owner(block, by, 0, True) for by in range(1, dense)]

    def send_rows(sent):
        return [sent[0]] + [shift_owner(sent[j], *steps[j], False) for j in range(1, len(steps))]

    def whole_router(sources):
        return pl.pallas_call(
            functools.partial(router_kernel, rows, piece),
            out_shape=jax.ShapeDtypeStruct((experts, width), BF16),
            in_specs=[SMEM] + [VMEM] * reps,
            out_specs=VMEM,
            compiler_params=params(),
            cost_estimate=took(1),
            name="router",
        )(plane.reshape(1), *sources)

    def apply_experts(here):
        size, count = here[0].shape[0], len(here)
        results = pl.pallas_call(
            functools.partial(experts_kernel, count),
            out_shape=[jax.ShapeDtypeStruct((size, width), BF16)] * count,
            in_specs=[VMEM] * (count + 3),
            out_specs=[VMEM] * count,
            scratch_shapes=[pltpu.VMEM((size * count, width), BF16)],
            compiler_params=params(),
            cost_estimate=took(4),
            name="experts",
        )(*here, w_gate, w_up, w_down)
        return results

    def shift_back(array, by, core_by, is_dense):
        pairs = []
        for y in range(Y_SIZE):
            for x in range(x_size):
                for core_at in range(CORES):
                    along_x = is_dense ^ (mixed and core_at == 1)
                    there = moved(y, x, core_at, by, core_by, along_x)
                    pairs.append((there, (y * x_size + x) * CORES + core_at))
        return lax.ppermute(array, "expert", pairs)

    def combine(blocks, back, router_full, halves):
        sums = pl.pallas_call(
            functools.partial(combine_kernel, rows, cap, top, dense, halves),
            out_shape=[jax.ShapeDtypeStruct((rows, width), F32)]
            + [jax.ShapeDtypeStruct((rows // halves, width), BF16)] * (halves * (dense - 1)),
            in_specs=[VMEM] * (2 + dense + len(steps)),
            out_specs=[VMEM] * (1 + halves * (dense - 1)),
            compiler_params=params(),
            cost_estimate=took(2),
            name="combine",
        )(groups, router_full, *blocks, *back)
        return sums

    def return_sums(sums):
        halves = (len(sums) - 1) // (dense - 1)
        return [sums[0]] + [
            [shift_back(sums[1 + by * halves + h], by + 1, 0, True) for by in range(dense - 1)]
            for h in range(halves)
        ]

    def add_up(own, *lists):
        starts, parts = [], []
        for pieces in lists:
            size = rows // len(pieces)
            starts += [h * size for h in range(len(pieces))]
            parts += pieces
        return pl.pallas_call(
            functools.partial(add_kernel, starts),
            out_shape=jax.ShapeDtypeStruct((rows, width), BF16),
            in_specs=[VMEM] * (1 + len(parts)),
            out_specs=VMEM,
            compiler_params=params(),
            cost_estimate=took(1),
            name="add",
        )(own, *parts)

    last = reps - 1
    blocks = [send_blocks(packed)]
    sources = [packed]
    for _ in range(last):
        sources.append(shift_plane(sources[-1], 1))
    sent = select(blocks[0])
    here = send_rows(sent)
    mark = sent[0]
    back, travelling = [], []

    def combine_chunk(i, halves, *others):
        back[i][0] = after(back[i][0], *others)
        sums = combine(blocks[i], back[i], router_full, halves)
        return sums[0], return_sums(sums)

    def add_chunk(sums, *others):
        own = after(sums[0], *others)
        lists = [list(column) for column in zip(*sums[1:])]
        part = add_up(own, *lists, *([travelling] if travelling else []))
        travelling[:] = [shift_plane(part, 1)]
        return part

    def send_back(results, *others):
        back = [results[0]]
        for j in range(1, len(steps)):
            rows_back = after(results[j], back[1], *others[min(j - 2, 1)]) if others and j > 1 else results[j]
            back.append(shift_back(rows_back, *steps[j], False))
        return back

    sums = None
    blocks.append(send_blocks(after(sources[1], *here[1:3])))
    for i in range(reps):
        arrived = here
        if 0 < i < last:
            blocks[i + 1][0] = after(blocks[i + 1][0], mark, *sources[i + 2 : i + 3])
            sent = select(blocks[i + 1])
            mark = sent[0]
            here = send_rows([sent[0]] + [after(rows_out, *arrived) for rows_out in sent[1:]])
            if i + 2 <= last:
                blocks.append(send_blocks(after(sources[i + 2], mark, *arrived)))
        if i == 2:
            router_full = whole_router([after(sources[0], mark)] + sources[1:])
        if 1 < i < last:
            if sums:
                mark = add_chunk(sums, mark)
            mark, sums = combine_chunk(i - 1, 1, mark)
        arrived[0] = after(arrived[0], mark, *(back[i - 1][1:] if 1 < i < last else []))
        results = apply_experts(arrived)
        back.append(send_back(results) if 0 < i < last else list(results))
        mark = results[0]
        if i == 0:
            blocks[1][0] = after(blocks[1][0], mark)
            sent = select(blocks[1])
            mark = sent[0]
            here = send_rows(sent)
            blocks.append(send_blocks(after(sources[2], mark, here[1])))
        if i == last:
            mark = add_chunk(sums, mark)
            mark, sums = combine_chunk(i - 1, HALVES, mark)
            back[last] = send_back(results, [mark], [mark, *sums[1], *travelling])
    mark = add_chunk(sums, mark)
    mark, sums = combine_chunk(last, HALVES, mark)
    back[0] = send_back([back[0][0]] + [after(x, mark) for x in back[0][1:]])
    mark = add_chunk(sums)
    back[0][0] = after(back[0][0], mark)
    own = return_sums(combine(blocks[0], back[0], router_full, HALVES))
    return add_up(own[0], *[list(column) for column in zip(*own[1:])], travelling)


def solution(mesh):
    placed = (
        P(("rep", "expert"), None),
        P(),
        P("rep", None),
        P(("rep", "expert"), None),
        P(),
        P(("rep", "expert"), None, None),
        P(("rep", "expert"), None, None),
        P(("rep", "expert"), None, None),
    )
    return jax.shard_map(
        per_device,
        mesh=mesh,
        in_specs=placed,
        out_specs=P(("rep", "expert"), None),
        check_vma=False,
    )
```

```python
import functools

import jax
import jax.numpy as jnp
from jax import lax
from jax.experimental import pallas as pl
from jax.experimental.pallas import tpu as pltpu
from jax.sharding import PartitionSpec as P

BF16, F32, I32 = jnp.bfloat16, jnp.float32, jnp.int32
CORES = 2
Y_SIZE = 2
HALVES = 2
MIB = 1 << 20
SMEM = pl.BlockSpec(memory_space=pltpu.SMEM)
VMEM = pl.BlockSpec(memory_space=pltpu.VMEM)
HBM = pl.BlockSpec(memory_space=pltpu.HBM)


def round_up(number, step):
    return -(-number // step) * step


def took(microseconds):
    return pl.CostEstimate(flops=int(microseconds * 1e9), bytes_accessed=0, transcendentals=0)


def params():
    return pltpu.CompilerParams(vmem_limit_bytes=12 * MIB)


def pack_kernel(piece, tokens, gain, routes, router, out_ref):
    rows, width = tokens.shape
    top = routes.shape[0]
    depth = router.shape[1]
    extra = out_ref.shape[0] - rows
    values = tokens[...].astype(F32)
    scale = lax.rsqrt(jnp.mean(values * values, axis=-1, keepdims=True) + 1e-06)
    out_ref[:rows, :] = (values * scale * gain[...]).astype(BF16)
    spread = jnp.concatenate(
        [router[q * piece : (q + 1) * piece, :].astype(F32) for q in range(width // depth)], axis=1
    )
    parts = [jnp.concatenate([routes[...].astype(F32), jnp.zeros((top, width - rows), F32)], axis=1), spread]
    if extra > top + piece:
        parts.insert(1, jnp.zeros((extra - top - piece, width), F32))
    out_ref[rows:, :] = jnp.concatenate(parts, axis=0).astype(BF16)


def router_kernel(rows, piece, plane_ref, *refs):
    blocks, out_ref = refs[:-1], refs[-1]
    pieces = len(blocks)
    depth = out_ref.shape[1] // pieces
    for d, block in enumerate(blocks):
        start = pl.multiple_of(lax.rem(plane_ref[0] - d + pieces, pieces) * depth, depth)
        last = block[rows:, :].astype(F32)[-piece:]
        out_ref[:, pl.ds(start, depth)] = jnp.concatenate(
            [last[:, q * depth : (q + 1) * depth] for q in range(pieces)], axis=0
        ).astype(BF16)


def membership(routes, experts, rows):
    names = lax.broadcasted_iota(I32, (experts, rows), 0).astype(F32)
    member = names == routes[0:1, :]
    for k in range(1, routes.shape[0]):
        member = member | (names == routes[k : k + 1, :])
    return member


def positions(member, groups_ref, rows):
    mine = jnp.dot(
        groups_ref[...].astype(BF16), jnp.where(member, 1.0, 0.0).astype(BF16), preferred_element_type=F32
    )
    earlier = lax.broadcasted_iota(I32, (rows, rows), 0) < lax.broadcasted_iota(I32, (rows, rows), 1)
    rank = jnp.dot(
        mine.astype(BF16), jnp.where(earlier, 1.0, 0.0).astype(BF16), preferred_element_type=F32
    )
    return jnp.where(mine > 0, rank, -1.0)


def select_kernel(rows, cap, top, groups_ref, *refs):
    groups, experts = groups_ref.shape
    blocks, outs = refs[:-groups], refs[-groups:]
    slot = lax.broadcasted_iota(I32, (cap, rows), 0).astype(F32)
    for i, block in enumerate(blocks):
        routes = block[rows : rows + 16, :rows].astype(F32)[:top]
        place = positions(membership(routes, experts, rows), groups_ref, rows)
        pick = jnp.concatenate(
            [jnp.where(slot == place[j : j + 1, :], 1.0, 0.0) for j in range(groups)], axis=0
        ).astype(BF16)
        found = jnp.dot(pick, block[:rows, :], preferred_element_type=F32).astype(BF16)
        for j in range(groups):
            outs[j][i * cap : (i + 1) * cap, :] = found[j * cap : (j + 1) * cap, :]


def experts_kernel(groups, *refs):
    ins, (gate_ref, up_ref, down_ref) = refs[:groups], refs[groups : groups + 3]
    outs, (stacked,) = refs[groups + 3 : -1], refs[-1:]
    size = ins[0].shape[0]
    hidden_width = gate_ref.shape[2]
    for j in range(groups):
        stacked[j * size : (j + 1) * size, :] = ins[j][...]
    gate = jnp.dot(stacked[...], gate_ref[0], preferred_element_type=F32)
    up = jnp.dot(stacked[...], up_ref[0], preferred_element_type=F32)
    hidden = (gate / (1.0 + jnp.exp(-gate)) * up).astype(BF16)
    product = jnp.dot(hidden, down_ref[0], preferred_element_type=F32).astype(BF16)
    for j in range(groups):
        outs[j][...] = product[j * size : (j + 1) * size, :]


def combine_kernel(rows, cap, top, dense, halves, groups_ref, router_ref, *refs):
    groups, experts = groups_ref.shape
    blocks, results, outs = refs[:dense], refs[dense : dense + groups], refs[dense + groups :]
    slot = lax.broadcasted_iota(I32, (cap, rows), 0).astype(F32)
    for i, block in enumerate(blocks):
        routes = block[rows : rows + 16, :rows].astype(F32)[:top]
        member = membership(routes, experts, rows)
        place = positions(member, groups_ref, rows)
        logits = lax.dot_general(
            router_ref[...], block[:rows, :], (((1,), (1,)), ((), ())), preferred_element_type=F32
        )
        powers = jnp.where(member, jnp.exp(logits), 0.0)
        shares = powers / jnp.sum(powers, axis=0, keepdims=True)
        own = jnp.dot(
            groups_ref[...], shares, preferred_element_type=F32, precision=lax.Precision.HIGHEST
        )
        weights = jnp.concatenate(
            [jnp.where(slot == place[j : j + 1, :], own[j : j + 1, :], 0.0) for j in range(groups)], axis=0
        )
        coarse = weights.astype(BF16)
        fine = (weights - coarse.astype(F32)).astype(BF16)
        found = jnp.concatenate(
            [result[i * cap : (i + 1) * cap, :] for result in results], axis=0
        )
        down = (((0,), (0,)), ((), ()))
        summed = lax.dot_general(coarse, found, down, preferred_element_type=F32)
        summed = summed + lax.dot_general(fine, found, down, preferred_element_type=F32)
        parts = outs[:1] if i == 0 else outs[1 + (i - 1) * halves : 1 + i * halves]
        size = rows // len(parts)
        for h, part in enumerate(parts):
            part[...] = summed[h * size : (h + 1) * size].astype(part.dtype)


def add_kernel(starts, own, *refs):
    out_ref = refs[-1]
    cuts = sorted(set(starts)) + [own.shape[0]]
    for low, high in zip(cuts[:-1], cuts[1:]):
        part = own[low:high, :]
        for start, ref in zip(starts, refs[:-1]):
            if start <= low < start + ref.shape[0]:
                part = part + ref[low - start : high - start, :].astype(F32)
        out_ref[low:high, :] = part.astype(BF16)


def per_device(tokens, norm_gain, router, routes, placement, w_gate, w_up, w_down):
    rows, width = tokens.shape
    top = routes.shape[1]
    experts = placement.shape[0]
    reps = lax.axis_size("rep")
    owners = lax.axis_size("expert")
    x_size = owners // (Y_SIZE * CORES)
    cap = round_up(3 * rows * top // (2 * experts), 16)
    plane = lax.axis_index("rep")
    owner = lax.axis_index("expert")
    depth = router.shape[0]
    piece = experts // reps
    extra = round_up(top + piece, 16)
    mixed = x_size == Y_SIZE
    dense = x_size
    steps = [(by, core_by) for by in range(Y_SIZE) for core_by in range(CORES)]

    def moved(y, x, core, by, core_by, along_x):
        if along_x:
            x = (x + by) % x_size
        else:
            y = (y + by) % Y_SIZE
        return (y * x_size + x) * CORES + (core ^ core_by)

    def shift_owner(array, by, core_by, is_dense):
        pairs = []
        for y in range(Y_SIZE):
            for x in range(x_size):
                for core in range(CORES):
                    along_x = is_dense ^ (mixed and core == 1)
                    there = moved(y, x, core, abs(by), core_by, along_x)
                    pairs.append(((y * x_size + x) * CORES + core, there))
        return lax.ppermute(array, "expert", pairs if by >= 0 else [(b, a) for a, b in pairs])

    def shift_plane(array, by):
        return lax.ppermute(array, "rep", [(r, (r + by) % reps) for r in range(reps)])

    core = owner % CORES
    x_at = owner // CORES % x_size
    y_at = owner // CORES // x_size
    slots = []
    for by, core_by in steps:
        there = moved(y_at, x_at, core, by, core_by, False)
        if mixed:
            there = jnp.where(core == 1, moved(y_at, x_at, core, by, core_by, True), there)
        slots.append(plane * owners + there)
    groups = (placement[None, :] == jnp.stack(slots)[:, None]).astype(F32)

    shapes = [(rows, width), (1, width), (top, rows), (experts, depth)]
    packed = pl.pallas_call(
        functools.partial(pack_kernel, piece),
        out_shape=jax.ShapeDtypeStruct((rows + extra, width), BF16),
        in_specs=[pl.BlockSpec(shape, lambda i: (0, 0)) for shape in shapes],
        out_specs=VMEM,
        grid=(1,),
        compiler_params=params(),
        name="pack",
    )(tokens, norm_gain.reshape(1, width), routes.T, router.T)

    def after(array, *others):
        return lax.optimization_barrier((array, *others))[0]

    def after_all(arrays, *others):
        return lax.optimization_barrier((tuple(arrays), *others))[0]

    def select(blocks):
        return pl.pallas_call(
            functools.partial(select_kernel, rows, cap, top),
            out_shape=[jax.ShapeDtypeStruct((dense * cap, width), BF16)] * len(steps),
            in_specs=[VMEM] * (1 + dense),
            out_specs=[VMEM] * len(steps),
            compiler_params=params(),
            cost_estimate=took(1),
            name="select",
        )(groups, *blocks)

    def send_blocks(block):
        return [block] + [shift_owner(block, by, 0, True) for by in range(1, dense)]

    def send_rows(sent):
        return [sent[0]] + [shift_owner(sent[j], *steps[j], False) for j in range(1, len(steps))]

    def whole_router(sources):
        return pl.pallas_call(
            functools.partial(router_kernel, rows, piece),
            out_shape=jax.ShapeDtypeStruct((experts, width), BF16),
            in_specs=[SMEM] + [VMEM] * reps,
            out_specs=VMEM,
            compiler_params=params(),
            cost_estimate=took(1),
            name="router",
        )(plane.reshape(1), *sources)

    def apply_experts(here):
        size, count = here[0].shape[0], len(here)
        results = pl.pallas_call(
            functools.partial(experts_kernel, count),
            out_shape=[jax.ShapeDtypeStruct((size, width), BF16)] * count,
            in_specs=[VMEM] * (count + 3),
            out_specs=[VMEM] * count,
            scratch_shapes=[pltpu.VMEM((size * count, width), BF16)],
            compiler_params=params(),
            cost_estimate=took(4),
            name="experts",
        )(*here, w_gate, w_up, w_down)
        return results

    def shift_back(array, by, core_by, is_dense):
        pairs = []
        for y in range(Y_SIZE):
            for x in range(x_size):
                for core_at in range(CORES):
                    along_x = is_dense ^ (mixed and core_at == 1)
                    there = moved(y, x, core_at, by, core_by, along_x)
                    pairs.append((there, (y * x_size + x) * CORES + core_at))
        return lax.ppermute(array, "expert", pairs)

    def combine(blocks, back, router_full, halves):
        sums = pl.pallas_call(
            functools.partial(combine_kernel, rows, cap, top, dense, halves),
            out_shape=[jax.ShapeDtypeStruct((rows, width), F32)]
            + [jax.ShapeDtypeStruct((rows // halves, width), BF16)] * (halves * (dense - 1)),
            in_specs=[VMEM] * (2 + dense + len(steps)),
            out_specs=[VMEM] * (1 + halves * (dense - 1)),
            compiler_params=params(),
            cost_estimate=took(2),
            name="combine",
        )(groups, router_full, *blocks, *back)
        return sums

    def return_sums(sums):
        halves = (len(sums) - 1) // (dense - 1)
        return [sums[0]] + [
            [shift_back(sums[1 + by * halves + h], by + 1, 0, True) for by in range(dense - 1)]
            for h in range(halves)
        ]

    def add_up(own, *lists):
        starts, parts = [], []
        for pieces in lists:
            size = rows // len(pieces)
            starts += [h * size for h in range(len(pieces))]
            parts += pieces
        return pl.pallas_call(
            functools.partial(add_kernel, starts),
            out_shape=jax.ShapeDtypeStruct((rows, width), BF16),
            in_specs=[VMEM] * (1 + len(parts)),
            out_specs=VMEM,
            compiler_params=params(),
            cost_estimate=took(1),
            name="add",
        )(own, *parts)

    last = reps - 1
    blocks = [send_blocks(packed)]
    sources = [packed]
    for _ in range(last):
        sources.append(shift_plane(sources[-1], 1))
    sent = select(blocks[0])
    here = send_rows(sent)
    mark = sent[0]
    back, travelling = [], []

    def combine_chunk(i, halves, *others):
        back[i][0] = after(back[i][0], *others)
        sums = combine(blocks[i], back[i], router_full, halves)
        return sums[0], return_sums(sums)

    def add_chunk(sums, *others):
        own = after(sums[0], *others)
        lists = [list(column) for column in zip(*sums[1:])]
        part = add_up(own, *lists, *([travelling] if travelling else []))
        travelling[:] = [shift_plane(part, 1)]
        return part

    def send_back(results, *others):
        back = [results[0]]
        for j in range(1, len(steps)):
            rows_back = after(results[j], back[1], *others[min(j - 2, 1)]) if others and j > 1 else results[j]
            back.append(shift_back(rows_back, *steps[j], False))
        return back

    sums = None
    blocks.append(send_blocks(after(sources[1], *here[1:3])))
    for i in range(reps):
        arrived = here
        if 0 < i < last:
            blocks[i + 1][0] = after(blocks[i + 1][0], mark, *sources[i + 2 : i + 3])
            sent = select(blocks[i + 1])
            mark = sent[0]
            here = send_rows([sent[0]] + [after(rows_out, *arrived) for rows_out in sent[1:]])
            if i + 2 <= last:
                blocks.append(send_blocks(after(sources[i + 2], mark, *arrived)))
        if i == 2:
            router_full = whole_router([after(sources[0], mark)] + sources[1:])
        if 1 < i < last:
            if sums:
                mark = add_chunk(sums, mark)
            mark, sums = combine_chunk(i - 1, 1, mark)
        arrived[0] = after(arrived[0], mark, *(back[i - 1][1:] if 1 < i < last else []))
        results = apply_experts(arrived)
        back.append(send_back(results) if 0 < i < last else list(results))
        mark = results[0]
        if i == 0:
            blocks[1][0] = after(blocks[1][0], mark, sources[2])
            sent = select(blocks[1])
            mark = sent[0]
            here = send_rows(sent)
            blocks.append(send_blocks(after(sources[2], mark, here[1])))
        if i == last:
            mark = add_chunk(sums, mark)
            mark, sums = combine_chunk(i - 1, HALVES, mark)
            back[last] = send_back(results, [mark], [mark, *sums[1], *travelling])
    mark = add_chunk(sums, mark)
    mark, sums = combine_chunk(last, HALVES, mark)
    back[0] = send_back([back[0][0]] + [after(x, mark) for x in back[0][1:]])
    mark = add_chunk(sums)
    back[0][0] = after(back[0][0], mark)
    own = return_sums(combine(blocks[0], back[0], router_full, HALVES))
    return add_up(own[0], *[list(column) for column in zip(*own[1:])], travelling)


def solution(mesh):
    placed = (
        P(("rep", "expert"), None),
        P(),
        P("rep", None),
        P(("rep", "expert"), None),
        P(),
        P(("rep", "expert"), None, None),
        P(("rep", "expert"), None, None),
        P(("rep", "expert"), None, None),
    )
    return jax.shard_map(
        per_device,
        mesh=mesh,
        in_specs=placed,
        out_specs=P(("rep", "expert"), None),
        check_vma=False,
    )
```

```python
import functools

import jax
import jax.numpy as jnp
from jax import lax
from jax.experimental import pallas as pl
from jax.experimental.pallas import tpu as pltpu
from jax.sharding import PartitionSpec as P

BF16, F32, I32 = jnp.bfloat16, jnp.float32, jnp.int32
CORES = 2
Y_SIZE = 2
HALVES = 2
MIB = 1 << 20
SMEM = pl.BlockSpec(memory_space=pltpu.SMEM)
VMEM = pl.BlockSpec(memory_space=pltpu.VMEM)
HBM = pl.BlockSpec(memory_space=pltpu.HBM)


def round_up(number, step):
    return -(-number // step) * step


def took(microseconds):
    return pl.CostEstimate(flops=int(microseconds * 1e9), bytes_accessed=0, transcendentals=0)


def params():
    return pltpu.CompilerParams(vmem_limit_bytes=12 * MIB)


def pack_kernel(piece, tokens, gain, routes, router, out_ref):
    rows, width = tokens.shape
    top = routes.shape[0]
    depth = router.shape[1]
    extra = out_ref.shape[0] - rows
    values = tokens[...].astype(F32)
    scale = lax.rsqrt(jnp.mean(values * values, axis=-1, keepdims=True) + 1e-06)
    out_ref[:rows, :] = (values * scale * gain[...]).astype(BF16)
    spread = jnp.concatenate(
        [router[q * piece : (q + 1) * piece, :].astype(F32) for q in range(width // depth)], axis=1
    )
    parts = [jnp.concatenate([routes[...].astype(F32), jnp.zeros((top, width - rows), F32)], axis=1), spread]
    if extra > top + piece:
        parts.insert(1, jnp.zeros((extra - top - piece, width), F32))
    out_ref[rows:, :] = jnp.concatenate(parts, axis=0).astype(BF16)


def router_kernel(rows, piece, plane_ref, *refs):
    blocks, out_ref = refs[:-1], refs[-1]
    pieces = len(blocks)
    depth = out_ref.shape[1] // pieces
    for d, block in enumerate(blocks):
        start = pl.multiple_of(lax.rem(plane_ref[0] - d + pieces, pieces) * depth, depth)
        last = block[rows:, :].astype(F32)[-piece:]
        out_ref[:, pl.ds(start, depth)] = jnp.concatenate(
            [last[:, q * depth : (q + 1) * depth] for q in range(pieces)], axis=0
        ).astype(BF16)


def membership(routes, experts, rows):
    names = lax.broadcasted_iota(I32, (experts, rows), 0).astype(F32)
    member = names == routes[0:1, :]
    for k in range(1, routes.shape[0]):
        member = member | (names == routes[k : k + 1, :])
    return member


def positions(member, groups_ref, rows):
    mine = jnp.dot(
        groups_ref[...].astype(BF16), jnp.where(member, 1.0, 0.0).astype(BF16), preferred_element_type=F32
    )
    earlier = lax.broadcasted_iota(I32, (rows, rows), 0) < lax.broadcasted_iota(I32, (rows, rows), 1)
    rank = jnp.dot(
        mine.astype(BF16), jnp.where(earlier, 1.0, 0.0).astype(BF16), preferred_element_type=F32
    )
    return jnp.where(mine > 0, rank, -1.0)


def select_kernel(rows, cap, top, groups_ref, *refs):
    groups, experts = groups_ref.shape
    blocks, outs = refs[:-groups], refs[-groups:]
    slot = lax.broadcasted_iota(I32, (cap, rows), 0).astype(F32)
    for i, block in enumerate(blocks):
        routes = block[rows : rows + 16, :rows].astype(F32)[:top]
        place = positions(membership(routes, experts, rows), groups_ref, rows)
        pick = jnp.concatenate(
            [jnp.where(slot == place[j : j + 1, :], 1.0, 0.0) for j in range(groups)], axis=0
        ).astype(BF16)
        found = jnp.dot(pick, block[:rows, :], preferred_element_type=F32).astype(BF16)
        for j in range(groups):
            outs[j][i * cap : (i + 1) * cap, :] = found[j * cap : (j + 1) * cap, :]


def experts_kernel(groups, *refs):
    ins, (gate_ref, up_ref, down_ref) = refs[:groups], refs[groups : groups + 3]
    outs, (stacked,) = refs[groups + 3 : -1], refs[-1:]
    size = ins[0].shape[0]
    hidden_width = gate_ref.shape[2]
    for j in range(groups):
        stacked[j * size : (j + 1) * size, :] = ins[j][...]
    gate = jnp.dot(stacked[...], gate_ref[0], preferred_element_type=F32)
    up = jnp.dot(stacked[...], up_ref[0], preferred_element_type=F32)
    hidden = (gate / (1.0 + jnp.exp(-gate)) * up).astype(BF16)
    product = jnp.dot(hidden, down_ref[0], preferred_element_type=F32).astype(BF16)
    for j in range(groups):
        outs[j][...] = product[j * size : (j + 1) * size, :]


def combine_kernel(rows, cap, top, dense, halves, groups_ref, router_ref, *refs):
    groups, experts = groups_ref.shape
    blocks, results, outs = refs[:dense], refs[dense : dense + groups], refs[dense + groups :]
    slot = lax.broadcasted_iota(I32, (cap, rows), 0).astype(F32)
    for i, block in enumerate(blocks):
        routes = block[rows : rows + 16, :rows].astype(F32)[:top]
        member = membership(routes, experts, rows)
        place = positions(member, groups_ref, rows)
        logits = lax.dot_general(
            router_ref[...], block[:rows, :], (((1,), (1,)), ((), ())), preferred_element_type=F32
        )
        powers = jnp.where(member, jnp.exp(logits), 0.0)
        shares = powers / jnp.sum(powers, axis=0, keepdims=True)
        own = jnp.dot(
            groups_ref[...], shares, preferred_element_type=F32, precision=lax.Precision.HIGHEST
        )
        weights = jnp.concatenate(
            [jnp.where(slot == place[j : j + 1, :], own[j : j + 1, :], 0.0) for j in range(groups)], axis=0
        )
        coarse = weights.astype(BF16)
        fine = (weights - coarse.astype(F32)).astype(BF16)
        found = jnp.concatenate(
            [result[i * cap : (i + 1) * cap, :] for result in results], axis=0
        )
        down = (((0,), (0,)), ((), ()))
        summed = lax.dot_general(coarse, found, down, preferred_element_type=F32)
        summed = summed + lax.dot_general(fine, found, down, preferred_element_type=F32)
        parts = outs[:1] if i == 0 else outs[1 + (i - 1) * halves : 1 + i * halves]
        size = rows // len(parts)
        for h, part in enumerate(parts):
            part[...] = summed[h * size : (h + 1) * size].astype(part.dtype)


def add_kernel(starts, own, *refs):
    out_ref = refs[-1]
    cuts = sorted(set(starts)) + [own.shape[0]]
    for low, high in zip(cuts[:-1], cuts[1:]):
        part = own[low:high, :]
        for start, ref in zip(starts, refs[:-1]):
            if start <= low < start + ref.shape[0]:
                part = part + ref[low - start : high - start, :].astype(F32)
        out_ref[low:high, :] = part.astype(BF16)


def per_device(tokens, norm_gain, router, routes, placement, w_gate, w_up, w_down):
    rows, width = tokens.shape
    top = routes.shape[1]
    experts = placement.shape[0]
    reps = lax.axis_size("rep")
    owners = lax.axis_size("expert")
    x_size = owners // (Y_SIZE * CORES)
    cap = round_up(3 * rows * top // (2 * experts), 16)
    plane = lax.axis_index("rep")
    owner = lax.axis_index("expert")
    depth = router.shape[0]
    piece = experts // reps
    extra = round_up(top + piece, 16)
    mixed = x_size == Y_SIZE
    dense = x_size
    steps = [(by, core_by) for by in range(Y_SIZE) for core_by in range(CORES)]

    def moved(y, x, core, by, core_by, along_x):
        if along_x:
            x = (x + by) % x_size
        else:
            y = (y + by) % Y_SIZE
        return (y * x_size + x) * CORES + (core ^ core_by)

    def shift_owner(array, by, core_by, is_dense):
        pairs = []
        for y in range(Y_SIZE):
            for x in range(x_size):
                for core in range(CORES):
                    along_x = is_dense ^ (mixed and core == 1)
                    there = moved(y, x, core, abs(by), core_by, along_x)
                    pairs.append(((y * x_size + x) * CORES + core, there))
        return lax.ppermute(array, "expert", pairs if by >= 0 else [(b, a) for a, b in pairs])

    def shift_plane(array, by):
        return lax.ppermute(array, "rep", [(r, (r + by) % reps) for r in range(reps)])

    core = owner % CORES
    x_at = owner // CORES % x_size
    y_at = owner // CORES // x_size
    slots = []
    for by, core_by in steps:
        there = moved(y_at, x_at, core, by, core_by, False)
        if mixed:
            there = jnp.where(core == 1, moved(y_at, x_at, core, by, core_by, True), there)
        slots.append(plane * owners + there)
    groups = (placement[None, :] == jnp.stack(slots)[:, None]).astype(F32)

    shapes = [(rows, width), (1, width), (top, rows), (experts, depth)]
    packed = pl.pallas_call(
        functools.partial(pack_kernel, piece),
        out_shape=jax.ShapeDtypeStruct((rows + extra, width), BF16),
        in_specs=[pl.BlockSpec(shape, lambda i: (0, 0)) for shape in shapes],
        out_specs=VMEM,
        grid=(1,),
        compiler_params=params(),
        name="pack",
    )(tokens, norm_gain.reshape(1, width), routes.T, router.T)

    def after(array, *others):
        return lax.optimization_barrier((array, *others))[0]

    def after_all(arrays, *others):
        return lax.optimization_barrier((tuple(arrays), *others))[0]

    def select(blocks):
        return pl.pallas_call(
            functools.partial(select_kernel, rows, cap, top),
            out_shape=[jax.ShapeDtypeStruct((dense * cap, width), BF16)] * len(steps),
            in_specs=[VMEM] * (1 + dense),
            out_specs=[VMEM] * len(steps),
            compiler_params=params(),
            cost_estimate=took(1),
            name="select",
        )(groups, *blocks)

    def send_blocks(block):
        return [block] + [shift_owner(block, by, 0, True) for by in range(1, dense)]

    def send_rows(sent):
        return [sent[0]] + [shift_owner(sent[j], *steps[j], False) for j in range(1, len(steps))]

    def whole_router(sources):
        return pl.pallas_call(
            functools.partial(router_kernel, rows, piece),
            out_shape=jax.ShapeDtypeStruct((experts, width), BF16),
            in_specs=[SMEM] + [VMEM] * reps,
            out_specs=VMEM,
            compiler_params=params(),
            cost_estimate=took(1),
            name="router",
        )(plane.reshape(1), *sources)

    def apply_experts(here):
        size, count = here[0].shape[0], len(here)
        results = pl.pallas_call(
            functools.partial(experts_kernel, count),
            out_shape=[jax.ShapeDtypeStruct((size, width), BF16)] * count,
            in_specs=[VMEM] * (count + 3),
            out_specs=[VMEM] * count,
            scratch_shapes=[pltpu.VMEM((size * count, width), BF16)],
            compiler_params=params(),
            cost_estimate=took(4),
            name="experts",
        )(*here, w_gate, w_up, w_down)
        return results

    def shift_back(array, by, core_by, is_dense):
        pairs = []
        for y in range(Y_SIZE):
            for x in range(x_size):
                for core_at in range(CORES):
                    along_x = is_dense ^ (mixed and core_at == 1)
                    there = moved(y, x, core_at, by, core_by, along_x)
                    pairs.append((there, (y * x_size + x) * CORES + core_at))
        return lax.ppermute(array, "expert", pairs)

    def combine(blocks, back, router_full, halves):
        sums = pl.pallas_call(
            functools.partial(combine_kernel, rows, cap, top, dense, halves),
            out_shape=[jax.ShapeDtypeStruct((rows, width), F32)]
            + [jax.ShapeDtypeStruct((rows // halves, width), BF16)] * (halves * (dense - 1)),
            in_specs=[VMEM] * (2 + dense + len(steps)),
            out_specs=[VMEM] * (1 + halves * (dense - 1)),
            compiler_params=params(),
            cost_estimate=took(2),
            name="combine",
        )(groups, router_full, *blocks, *back)
        return sums

    def return_sums(sums):
        halves = (len(sums) - 1) // (dense - 1)
        return [sums[0]] + [
            [shift_back(sums[1 + by * halves + h], by + 1, 0, True) for by in range(dense - 1)]
            for h in range(halves)
        ]

    def add_up(own, *lists):
        starts, parts = [], []
        for pieces in lists:
            size = rows // len(pieces)
            starts += [h * size for h in range(len(pieces))]
            parts += pieces
        return pl.pallas_call(
            functools.partial(add_kernel, starts),
            out_shape=jax.ShapeDtypeStruct((rows, width), BF16),
            in_specs=[VMEM] * (1 + len(parts)),
            out_specs=VMEM,
            compiler_params=params(),
            cost_estimate=took(1),
            name="add",
        )(own, *parts)

    last = reps - 1
    blocks = [send_blocks(packed)]
    sources = [packed]
    for _ in range(last):
        sources.append(shift_plane(sources[-1], 1))
    sent = select(blocks[0])
    here = send_rows(sent)
    mark = sent[0]
    back, travelling = [], []

    def combine_chunk(i, halves, *others):
        back[i][0] = after(back[i][0], *others)
        sums = combine(blocks[i], back[i], router_full, halves)
        return sums[0], return_sums(sums)

    def add_chunk(sums, *others):
        own = after(sums[0], *others)
        lists = [list(column) for column in zip(*sums[1:])]
        part = add_up(own, *lists, *([travelling] if travelling else []))
        travelling[:] = [shift_plane(part, 1)]
        return part

    def send_back(results, *others):
        back = [results[0]]
        for j in range(1, len(steps)):
            rows_back = after(results[j], back[1], *others[min(j - 2, 1)]) if others and j > 1 else results[j]
            back.append(shift_back(rows_back, *steps[j], False))
        return back

    sums = None
    blocks.append(send_blocks(after(sources[1], *here[1:3])))
    for i in range(reps):
        arrived = here
        if 0 < i < last:
            blocks[i + 1][0] = after(blocks[i + 1][0], mark, *sources[i + 2 : i + 3])
            sent = select(blocks[i + 1])
            mark = sent[0]
            here = send_rows([sent[0]] + [after(rows_out, *arrived) for rows_out in sent[1:]])
            if i + 2 <= last:
                blocks.append(send_blocks(after(sources[i + 2], mark, *arrived)))
        if i == 2:
            router_full = whole_router([after(sources[0], mark)] + sources[1:])
        if 1 < i < last:
            if sums:
                mark = add_chunk(sums, mark)
            mark, sums = combine_chunk(i - 1, 1, mark)
        arrived[0] = after(arrived[0], mark, *(back[i - 1][1:] if 1 < i < last else []))
        results = apply_experts(arrived)
        back.append(send_back(results) if 0 < i < last else list(results))
        mark = results[0]
        if i == 0:
            blocks[1][0] = after(blocks[1][0], mark)
            sent = select(blocks[1])
            mark = sent[0]
            here = send_rows(sent)
            blocks.append(send_blocks(after(sources[2], mark, here[1])))
        if i == last:
            mark = add_chunk(sums, mark)
            mark, sums = combine_chunk(i - 1, HALVES, mark)
            back[last] = send_back(results, [mark], [mark, *sums[1], *travelling])
            ahead = [*sums[1], *sums[2]]
    mark = add_chunk(sums, mark)
    mark, sums = combine_chunk(last, HALVES, mark)
    own = back[0]
    for j in range(1, len(steps)):
        own[j] = shift_back(after(own[j], *(ahead if j < 3 else [mark, own[2]])), *steps[j], False)
    mark = add_chunk(sums)
    back[0][0] = after(back[0][0], mark)
    own = return_sums(combine(blocks[0], back[0], router_full, HALVES))
    return add_up(own[0], *[list(column) for column in zip(*own[1:])], travelling)


def solution(mesh):
    placed = (
        P(("rep", "expert"), None),
        P(),
        P("rep", None),
        P(("rep", "expert"), None),
        P(),
        P(("rep", "expert"), None, None),
        P(("rep", "expert"), None, None),
        P(("rep", "expert"), None, None),
    )
    return jax.shard_map(
        per_device,
        mesh=mesh,
        in_specs=placed,
        out_specs=P(("rep", "expert"), None),
        check_vma=False,
    )
```
